512 devices in a mesh: blk: 128 (over x_lo, y, z), grp: 4 (over x_hi, core).
Axes of the slice: x: 4 (x_hi: 2, x_lo: 2; x = x_hi * 2 + x_lo), y: 4, z: 16, core: 2. Of those that a mesh axis runs over, the one named last changes fastest.
Arguments:
- view_a: bfloat16 [98304, 1024], P(('blk', 'grp')), may hold values from -1 to 1
- view_b: bfloat16 [98304, 1024], P(('blk', 'grp')), may hold values from -1 to 1
- positive: int32 [98304], P(('blk', 'grp')), may hold values from 0 to 98303, as said below
Outputs:
- row_loss: float32 [98304], P(('blk', 'grp'))
- grad_a: float32 [98304, 1024], P(('blk', 'grp'))
- grad_b: float32 [98304, 1024], P(('blk', 'grp'))
The draws below stay inside these ranges and needn't reach their ends.
Inputs may be any that keep to these rules, and one draw needn't show every extreme that they name: Within each aligned block of 768 rows, positive is a permutation of that same block's row numbers.
All inputs are finite; a program needn't handle non-finite values.
Results may differ from the reference program's by a relative error of at most 0.0053.
Values may be sent and summed in bfloat16 or wider, within the bound.
A program may use at most 64 MiB of HBM per device.

```python
import jax
import jax.numpy as jnp
from jax import lax

D = 1024
ROWS_DEV = 192
SPAN = 2
BLOCK = 768
BATCH = 98304
N_BLK = 128
N_GRP = 4


def shared_keys(key):
    blocks = BATCH // BLOCK
    block_keys = jax.random.split(jax.random.fold_in(key, 101), blocks)
    perms = jax.vmap(lambda k: jax.random.permutation(k, BLOCK))(block_keys).astype(jnp.int32)
    order = (perms + (jnp.arange(blocks, dtype=jnp.int32) * BLOCK)[:, None]).reshape(BATCH)
    groups = max(BATCH // 384, 1)
    centres = jax.random.normal(jax.random.fold_in(key, 105), (groups, D), jnp.float32)
    member = jax.random.randint(jax.random.fold_in(key, 106), (BATCH,), 0, groups).astype(jnp.int32)
    base = jax.random.normal(jax.random.fold_in(key, 102), (BATCH, D), jnp.float32)
    values = (0.894 * centres[member] + 0.447 * base) * D ** (-0.5)
    return (order, values)


def draw_positive(key, part):
    order, values = shared_keys(key)
    return order


def draw_view_b(key, part):
    order, values = shared_keys(key)
    return jnp.clip(values, -1.0, 1.0).astype(jnp.bfloat16)


def draw_view_a(key, part):
    order, values = shared_keys(key)
    key = jax.random.fold_in(key, 3)
    target = jnp.clip(values, -1.0, 1.0)[order]
    noise = jax.random.normal(key, (BATCH, D), jnp.float32) * D ** (-0.5)
    result = 0.5 * target + 1.4 * noise
    return jnp.clip(result, -1.0, 1.0).astype(jnp.bfloat16)


def setup_inputs(seed: int = 0) -> dict:
    arg_keys = jax.random.split(jax.random.key(seed), 4)
    return {
        "view_a": draw_view_a(jax.random.fold_in(arg_keys[3], 71), 0),
        "view_b": draw_view_b(jax.random.fold_in(arg_keys[3], 71), 0),
        "positive": draw_positive(jax.random.fold_in(arg_keys[3], 71), 0),
    }


inverse_temp = 20.0


def reference(view_a, view_b, positive):
    block_rows = ROWS_DEV * N_GRP
    count = N_BLK
    reach = 2 * SPAN + 1
    a_blocks = view_a.reshape(count, block_rows, D)
    b_blocks = view_b.reshape(count, block_rows, D)
    pos_blocks = positive.reshape(count, block_rows)
    offsets = jnp.arange(-SPAN, SPAN + 1, dtype=jnp.int32)
    matched_sum = jnp.zeros((BATCH, D), jnp.float32).at[positive].add(view_a.astype(jnp.float32))
    keys_float = view_b.astype(jnp.float32)

    def step(accum, index):
        queries = a_blocks[index]
        targets = pos_blocks[index]
        where = ((index + offsets) % count).astype(jnp.int32)
        keys = b_blocks[where].reshape(reach * block_rows, D)
        scores = inverse_temp * jnp.dot(queries, keys.T, preferred_element_type=jnp.float32)
        peak = jnp.max(scores, axis=1)
        lse = peak + jnp.log(jnp.sum(jnp.exp(scores - peak[:, None]), axis=1))
        local = (targets - index * block_rows + SPAN * block_rows).astype(jnp.int32)
        matched = jnp.take_along_axis(scores, local[:, None], axis=1)[:, 0]
        weights = jnp.exp(scores - lse[:, None]).astype(jnp.bfloat16)
        grad_rows = inverse_temp * (jnp.dot(weights, keys, preferred_element_type=jnp.float32) - keys_float[targets])
        contrib = jnp.dot(weights.T, queries, preferred_element_type=jnp.float32).reshape(reach, block_rows, D)
        accum = accum.at[where].add(contrib)
        return accum, (lse - matched, grad_rows)

    start = jnp.zeros((count, block_rows, D), jnp.float32)
    accum, (losses, grads) = lax.scan(step, start, jnp.arange(count, dtype=jnp.int32))
    grad_b = inverse_temp * (accum.reshape(BATCH, D) - matched_sum)
    return losses.reshape(BATCH), grads.reshape(BATCH, D), grad_b
```

```python
import functools

import jax
import jax.numpy as jnp
from jax import lax
from jax.experimental import pallas as pl
from jax.experimental.pallas import tpu as pltpu
from jax.sharding import PartitionSpec as P

SPAN = 2
WINDOW = 2 * SPAN + 1
GROUPS = 4
CHUNKS = 2
inverse_temp = 20.0
MESH = pl.DeviceIdType.MESH
TOP = 32766.0


def encode(x):
    peak = jnp.max(jnp.abs(x), axis=0, keepdims=True)
    alive = peak > 1e-30
    scale = jnp.where(alive, TOP / jnp.where(alive, peak, 1.0), 0.0)
    codes = jnp.round(x * scale).astype(jnp.int32).astype(jnp.int16)
    return codes, jnp.where(alive, peak * (1.0 / TOP), 0.0)


def decode(codes, step):
    return codes.astype(jnp.int32).astype(jnp.float32) * step


def kernel(
    a_in, b_in, pos_in, loss_out, grad_a_out, grad_b_out,
    queries, keys, pos_buf, stat_buf, scores, weights, hits_buf,
    home, side, code1_out, step1_out, code1_in, step1_in, code2_out, step2_out, code2_in, step2_in,
    part, sib_in, codex_out, stepx_out, codex_in, stepx_in,
    load_sem, b_send, b_recv, a_send, a_recv, p_send, p_recv, s_send, s_recv,
    c_send, c_recv, t_send, t_recv, d_send, d_recv, x_send, x_recv,
):
    rows, width = a_in.shape
    block = rows * GROUPS
    cut = rows // CHUNKS
    blk = lax.axis_index("blk")
    grp = lax.axis_index("grp")
    blocks = lax.axis_size("blk")
    right = lax.rem(blk + 1, blocks)
    left = lax.rem(blk + blocks - 1, blocks)
    sib = grp + 1 - 2 * lax.rem(grp, 2)
    par = lax.rem(grp + 2, GROUPS)
    dia = lax.rem(sib + 2, GROUPS)
    ways = (right, left)
    peers = (sib, par, dia)

    def remote(src, dst, send, recv, to_blk, to_grp):
        return pltpu.make_async_remote_copy(
            src_ref=src, dst_ref=dst, send_sem=send, recv_sem=recv,
            device_id=(to_blk, to_grp), device_id_type=MESH,
        )

    load_b = pltpu.make_async_copy(b_in, keys.at[SPAN], load_sem.at[0])
    load_a = pltpu.make_async_copy(a_in, queries.at[grp], load_sem.at[1])
    load_b.start()
    load_a.start()
    pos_buf[grp] = jnp.zeros(pos_buf.shape[1:], jnp.int32)
    pos_buf[grp, 0:1, 0:rows] = pos_in[...] - blk * block

    barrier = pltpu.get_barrier_semaphore()
    for way in ways:
        pl.semaphore_signal(barrier, inc=1, device_id=(way, grp), device_id_type=MESH)
    for peer in peers:
        pl.semaphore_signal(barrier, inc=1, device_id=(blk, peer), device_id_type=MESH)
    pl.semaphore_wait(barrier, 5)
    load_b.wait()
    load_a.wait()

    def key_copy(hop, d, c):
        part_rows = pl.ds(c * cut, cut)
        src = SPAN if hop == 0 else (SPAN - 1, SPAN + 1)[d]
        dst = ((SPAN - 1, SPAN + 1), (SPAN - 2, SPAN + 2))[hop][d]
        return remote(
            keys.at[src, part_rows], keys.at[dst, part_rows],
            b_send.at[hop, d, c], b_recv.at[hop, d, c], ways[d], grp,
        )

    key_copies = {(h, d, c): key_copy(h, d, c) for h in range(2) for d in range(2) for c in range(CHUNKS)}
    for c in range(CHUNKS):
        for d in range(2):
            key_copies[0, d, c].start()
        if c == 0:
            to_par = remote(queries.at[grp], queries.at[grp], a_send.at[1], a_recv.at[1], blk, par)
            to_par.start()
            to_sib = remote(queries.at[grp], queries.at[grp], a_send.at[0], a_recv.at[0], blk, sib)
            to_sib.start()
    pos_copies = [
        remote(pos_buf.at[grp], pos_buf.at[grp], p_send.at[i], p_recv.at[i], blk, peer)
        for i, peer in enumerate(peers)
    ]
    for copy in pos_copies:
        copy.start()
    for c in range(CHUNKS):
        for d in range(2):
            key_copies[0, d, c].wait_recv()
            key_copies[1, d, c].start()
    to_par.wait_recv()
    onward = remote(queries.at[par], queries.at[par], a_send.at[2], a_recv.at[2], blk, sib)
    onward.start()
    to_sib.wait_recv()
    onward.wait_recv()
    for copy in pos_copies:
        copy.wait_recv()

    every_query = queries[...].reshape(block, width)

    def score(s, lo, size):
        scores[s, lo : lo + size, :] = inverse_temp * lax.dot_general(
            keys[s, lo : lo + size, :], every_query, (((1,), (1,)), ((), ())),
            preferred_element_type=jnp.float32,
        )

    for s in (SPAN, SPAN - 1, SPAN + 1):
        score(s, 0, rows)
    place = jnp.concatenate([pos_buf[t, 0:1, 0:rows] for t in range(GROUPS)], axis=1)
    own_rows = lax.broadcasted_iota(jnp.int32, (rows, block), 0) + grp * rows
    hits = own_rows == place
    hits_buf[...] = jnp.where(hits, 1.0, 0.0).astype(jnp.bfloat16)
    matched = jnp.sum(jnp.where(hits, scores[SPAN], 0.0), axis=0, keepdims=True)
    near = [SPAN, SPAN - 1, SPAN + 1]
    far = [SPAN - 2, SPAN + 2]
    peak3 = functools.reduce(jnp.maximum, [jnp.max(scores[s], axis=0, keepdims=True) for s in near])
    total3 = sum(jnp.sum(jnp.exp(scores[s] - peak3), axis=0, keepdims=True) for s in near)
    for c in range(CHUNKS):
        for d in range(2):
            key_copies[1, d, c].wait_recv()
            score(far[d], c * cut, cut)
    peak = functools.reduce(jnp.maximum, [peak3] + [jnp.max(scores[s], axis=0, keepdims=True) for s in far])
    total = total3 * jnp.exp(peak3 - peak)
    total = total + sum(jnp.sum(jnp.exp(scores[s] - peak), axis=0, keepdims=True) for s in far)

    stat_buf[grp] = jnp.zeros(stat_buf.shape[1:], jnp.float32)
    stat_buf[grp, 0:1, :] = peak
    stat_buf[grp, 1:2, :] = total
    stat_buf[grp, 2:3, :] = matched
    stat_copies = [
        remote(stat_buf.at[grp], stat_buf.at[grp], s_send.at[i], s_recv.at[i], blk, peer)
        for i, peer in enumerate(peers)
    ]
    for copy in stat_copies:
        copy.start()
    for copy in stat_copies:
        copy.wait_recv()
    peaks = [stat_buf[t, 0:1, :] for t in range(GROUPS)]
    peak = functools.reduce(jnp.maximum, peaks)
    total = sum(stat_buf[t, 1:2, :] * jnp.exp(peaks[t] - peak) for t in range(GROUPS))
    lse = peak + jnp.log(total)
    loss_out[...] = lse - sum(stat_buf[t, 2:3, :] for t in range(GROUPS))

    def weigh(s, lo, size):
        weights[s, lo : lo + size, :] = jnp.exp(scores[s, lo : lo + size, :] - lse).astype(jnp.bfloat16)

    def term(s, lo, size):
        weigh(s, lo, size)
        return jnp.dot(weights[s, lo : lo + size, :], every_query, preferred_element_type=jnp.float32)

    def code_copies(hop, d, c):
        codes = (code1_out, code2_out)[hop], (code1_in, code2_in)[hop]
        steps = (step1_out, step2_out)[hop], (step1_in, step2_in)[hop]
        part_rows = pl.ds(c * cut, cut)
        return (
            remote(codes[0].at[d, part_rows], codes[1].at[d, part_rows], c_send.at[hop, d, c], c_recv.at[hop, d, c], ways[d], grp),
            remote(steps[0].at[d, c], steps[1].at[d, c], t_send.at[hop, d, c], t_recv.at[hop, d, c], ways[d], grp),
        )

    back = {(h, d, c): code_copies(h, d, c) for h in range(2) for d in range(2) for c in range(CHUNKS)}

    def send_back(hop, d, c, value):
        codes_out, steps_out = ((code1_out, step1_out), (code2_out, step2_out))[hop]
        codes, step = encode(value)
        codes_out[d, c * cut : (c + 1) * cut, :] = codes
        steps_out[d, c] = step
        for copy in back[hop, d, c]:
            copy.start()

    def received(hop, d, c):
        for copy in back[hop, d, c]:
            copy.wait_recv()
        codes_in, steps_in = ((code1_in, step1_in), (code2_in, step2_in))[hop]
        return decode(codes_in[d, c * cut : (c + 1) * cut, :], steps_in[d, c])

    to_far, to_near = (SPAN + 2, SPAN - 2), (SPAN + 1, SPAN - 1)
    for c in range(CHUNKS):
        for d in range(2):
            send_back(0, d, c, term(to_far[d], c * cut, cut))
    for d in range(2):
        side[d] = term(to_near[d], 0, rows)
    home[...] = term(SPAN, 0, rows) - jnp.dot(hits_buf[...], every_query, preferred_element_type=jnp.float32)

    every_weight = weights[...].reshape(WINDOW * rows, block)
    window = keys[...].reshape(WINDOW * rows, width)
    across = (((0,), (0,)), ((), ()))
    query_part = lax.dot_general(every_weight, window, across, preferred_element_type=jnp.float32)
    query_part = query_part - lax.dot_general(
        hits_buf[...], keys[SPAN], across, preferred_element_type=jnp.float32
    )
    part[...] = query_part.reshape(GROUPS, rows, width)
    sib_copies = [
        remote(part.at[t], sib_in.at[i], d_send.at[i], d_recv.at[i], blk, sib)
        for i, t in ((1, dia), (0, sib))
    ]
    for copy in sib_copies:
        copy.start()

    for d in range(2):
        send_back(1, d, 0, side[d, 0:cut, :] + received(0, d, 0))
    for copy in sib_copies:
        copy.wait_recv()
    codes, step = encode(part[par] + sib_in[1])
    codex_out[...] = codes
    stepx_out[...] = step
    x_copies = (
        remote(codex_out, codex_in, x_send.at[0], x_recv.at[0], blk, par),
        remote(stepx_out, stepx_in, x_send.at[1], x_recv.at[1], blk, par),
    )
    for copy in x_copies:
        copy.start()
    for c in range(1, CHUNKS):
        for d in range(2):
            lo = c * cut
            send_back(1, d, c, side[d, lo : lo + cut, :] + received(0, d, c))
    for copy in x_copies:
        copy.wait_recv()
    grad_a_out[...] = inverse_temp * (part[grp] + sib_in[0] + decode(codex_in[...], stepx_in[...]))
    for c in range(CHUNKS):
        lo = c * cut
        grad_b_out[lo : lo + cut, :] = inverse_temp * (
            home[lo : lo + cut, :] + received(1, 0, c) + received(1, 1, c)
        )

    for copy in key_copies.values():
        copy.wait_send()
    for pair in back.values():
        for copy in pair:
            copy.wait_send()
    for copy in (to_par, to_sib, onward, *pos_copies, *stat_copies, *sib_copies, *x_copies):
        copy.wait_send()


def body(view_a, view_b, positive):
    rows, width = view_a.shape
    block = rows * GROUPS
    cut = rows // CHUNKS
    lanes = -(-rows // 128) * 128
    vmem = pl.BlockSpec(memory_space=pltpu.VMEM)
    hbm = pl.BlockSpec(memory_space=pl.ANY)
    dma = pltpu.SemaphoreType.DMA
    f32, bf16, i16 = jnp.float32, jnp.bfloat16, jnp.int16
    codes = pltpu.VMEM((2, rows, width), i16)
    steps = pltpu.VMEM((2, CHUNKS, 1, width), f32)
    loss, grad_a, grad_b = pl.pallas_call(
        kernel,
        out_shape=(
            jax.ShapeDtypeStruct((1, block), f32),
            jax.ShapeDtypeStruct((rows, width), f32),
            jax.ShapeDtypeStruct((rows, width), f32),
        ),
        in_specs=[hbm, hbm, vmem],
        out_specs=(vmem, vmem, vmem),
        scratch_shapes=[
            pltpu.VMEM((GROUPS, rows, width), bf16),
            pltpu.VMEM((WINDOW, rows, width), bf16),
            pltpu.VMEM((GROUPS, 8, lanes), jnp.int32),
            pltpu.VMEM((GROUPS, 8, block), f32),
            pltpu.VMEM((WINDOW, rows, block), f32),
            pltpu.VMEM((WINDOW, rows, block), bf16),
            pltpu.VMEM((rows, block), bf16),
            pltpu.VMEM((rows, width), f32),
            pltpu.VMEM((2, rows, width), f32),
            codes, steps, codes, steps, codes, steps, codes, steps,
            pltpu.VMEM((GROUPS, rows, width), f32),
            pltpu.VMEM((2, rows, width), f32),
            pltpu.VMEM((rows, width), i16),
            pltpu.VMEM((1, width), f32),
            pltpu.VMEM((rows, width), i16),
            pltpu.VMEM((1, width), f32),
            dma((2,)),
            dma((2, 2, CHUNKS)), dma((2, 2, CHUNKS)),
            dma((3,)), dma((3,)),
            dma((3,)), dma((3,)),
            dma((3,)), dma((3,)),
            dma((2, 2, CHUNKS)), dma((2, 2, CHUNKS)),
            dma((2, 2, CHUNKS)), dma((2, 2, CHUNKS)),
            dma((2,)), dma((2,)),
            dma((2,)), dma((2,)),
        ],
        compiler_params=pltpu.CompilerParams(
            collective_id=0, has_side_effects=True, vmem_limit_bytes=56 * 2**20
        ),
        cost_estimate=pl.CostEstimate(
            flops=2 * block * rows * width * 17, bytes_accessed=rows * width * 12,
            transcendentals=2 * WINDOW * rows * block,
        ),
    )(view_a, view_b, positive.reshape(1, rows))
    row_loss = lax.dynamic_slice_in_dim(loss[0], lax.axis_index("grp") * rows, rows, 0)
    return row_loss, grad_a, grad_b


def solution(mesh):
    in_specs = (P(("blk", "grp"), None), P(("blk", "grp"), None), P(("blk", "grp")))
    out_specs = (P(("blk", "grp")), P(("blk", "grp"), None), P(("blk", "grp"), None))
    return jax.shard_map(body, mesh=mesh, in_specs=in_specs, out_specs=out_specs, check_vma=False)
```

```python
import functools

import jax
import jax.numpy as jnp
from jax import lax
from jax.experimental import pallas as pl
from jax.experimental.pallas import tpu as pltpu
from jax.sharding import PartitionSpec as P

SPAN = 2
WINDOW = 2 * SPAN + 1
GROUPS = 4
CHUNKS = 4
DETOUR = ((0, 1), (2, 3))
ORDER = (2, 3, 0, 1)
inverse_temp = 20.0
MESH = pl.DeviceIdType.MESH
TOP = 32766.0


def encode(x):
    peak = jnp.max(jnp.abs(x), axis=0, keepdims=True)
    alive = peak > 1e-30
    scale = jnp.where(alive, TOP / jnp.where(alive, peak, 1.0), 0.0)
    codes = jnp.round(x * scale).astype(jnp.int32).astype(jnp.int16)
    return codes, jnp.where(alive, peak * (1.0 / TOP), 0.0)


def decode(codes, step):
    return codes.astype(jnp.int32).astype(jnp.float32) * step


def kernel(
    a_in, b_in, pos_in, loss_out, grad_a_out, grad_b_out,
    queries, keys, pos_buf, stat_buf, scores, weights, hits_buf, home,
    code1_out, step1_out, code1_in, step1_in, code2_out, step2_out, code2_in, step2_in,
    part, sib_in, codex_out, stepx_out, codex_in, stepx_in,
    load_sem, b_send, b_recv, a_send, a_recv, p_send, p_recv, s_send, s_recv,
    c_send, c_recv, t_send, t_recv, d_send, d_recv, x_send, x_recv,
):
    rows, width = a_in.shape
    block = rows * GROUPS
    cut = rows // CHUNKS
    near = (SPAN + 1) * rows
    every = WINDOW * rows
    blk = lax.axis_index("blk")
    grp = lax.axis_index("grp")
    blocks = lax.axis_size("blk")
    right = lax.rem(blk + 1, blocks)
    left = lax.rem(blk + blocks - 1, blocks)
    sib = grp + 1 - 2 * lax.rem(grp, 2)
    par = lax.rem(grp + 2, GROUPS)
    dia = lax.rem(sib + 2, GROUPS)
    peers = (sib, par, dia)

    half = blocks // 2
    spot = lax.rem(blk, half)
    is_last, is_first = spot == half - 1, spot == 0
    is_relay = jnp.logical_or(is_last, is_first)
    detour = (is_last, is_first)
    across_x = lax.rem(blk + half, blocks)
    relay_to = lax.rem(blk + jnp.where(is_last, half + 1, half - 1), blocks)
    relay_d = jnp.where(is_last, 0, 1)

    def route(hop, d, c):
        if c not in DETOUR[hop]:
            return False, (right, left)[d]
        return detour[d], jnp.where(detour[d], across_x, (right, left)[d])

    def pick(flag, a, b):
        return b if flag is False else jnp.where(flag, a, b)

    def remote(src, dst, send, recv, to_blk, to_grp):
        return pltpu.make_async_remote_copy(
            src_ref=src, dst_ref=dst, send_sem=send, recv_sem=recv,
            device_id=(to_blk, to_grp), device_id_type=MESH,
        )

    def span(lo, size):
        return pl.ds(pl.multiple_of(lo, 16), size)

    load_b = pltpu.make_async_copy(b_in, keys.at[pl.ds(0, rows)], load_sem.at[0])
    load_a = pltpu.make_async_copy(a_in, queries.at[grp], load_sem.at[1])
    load_b.start()
    load_a.start()

    barrier = pltpu.get_barrier_semaphore()

    def greet(to_blk, to_grp):
        pl.semaphore_signal(barrier, inc=1, device_id=(to_blk, to_grp), device_id_type=MESH)

    greet(right, grp)
    greet(left, grp)
    for peer in peers:
        greet(blk, peer)

    @pl.when(is_relay)
    def _():
        greet(across_x, grp)
        greet(relay_to, grp)

    pos_buf[grp] = jnp.zeros(pos_buf.shape[1:], jnp.int32)
    pos_buf[grp, 0:1, 0:rows] = pos_in[...] - blk * block
    pl.semaphore_wait(barrier, 5 + jnp.where(is_relay, 2, 0))
    load_b.wait()

    def key_place(hop, d, c):
        if hop == 0:
            lands = rows * (1 + d) + c * cut
        else:
            lands = near + (2 * ORDER.index(c) + d) * cut
        return lands, every + hop * rows + c * cut

    def key_send(hop, d, c):
        src = c * cut if hop == 0 else rows * (1 + d) + c * cut
        direct, held = key_place(hop, d, c)
        by_relay, to_blk = route(hop, d, c)
        return remote(
            keys.at[pl.ds(src, cut)], keys.at[span(pick(by_relay, held, direct), cut)],
            b_send.at[hop, d, c], b_recv.at[hop, pick(by_relay, 2, d), c], to_blk, grp,
        )

    def key_wait(hop, d, c):
        place = keys.at[pl.ds(key_place(hop, d, c)[0], cut)]
        remote(place, place, b_send.at[hop, d, c], b_recv.at[hop, d, c], right, grp).wait_recv()

    def key_relay(hop, c):
        held = keys.at[pl.ds(key_place(hop, 0, c)[1], cut)]
        lands = jnp.where(is_last, key_place(hop, 0, c)[0], key_place(hop, 1, c)[0])
        return ((
            remote(held, held, b_send.at[hop, 2, c], b_recv.at[hop, 2, c], relay_to, grp),
            remote(held, keys.at[span(lands, cut)], b_send.at[hop, 2, c], b_recv.at[hop, relay_d, c], relay_to, grp),
        ),)

    def relay(hop, c, copies):
        if c not in DETOUR[hop]:
            return

        @pl.when(is_relay)
        def _():
            for arriving, _ in copies(hop, c):
                arriving.wait_recv()
            for _, leaving in copies(hop, c):
                leaving.start()

    key_sends = {(h, d, c): key_send(h, d, c) for h in range(2) for d in range(2) for c in range(CHUNKS)}
    middle_row = rows // 2
    query_rows = [pl.ds(i * middle_row, middle_row) for i in range(2)]
    to_par = [
        remote(queries.at[grp, r], queries.at[grp, r], a_send.at[1 + i], a_recv.at[1 + i], blk, par)
        for i, r in enumerate(query_rows)
    ]
    to_sib = remote(queries.at[grp], queries.at[grp], a_send.at[0], a_recv.at[0], blk, sib)
    for c in range(CHUNKS):
        for d in range(2):
            key_sends[0, d, c].start()
    load_a.wait()
    to_par[0].start()
    to_sib.start()

    @pl.when(jnp.logical_not(is_relay))
    def _():
        to_par[1].start()

    pos_copies = [
        remote(pos_buf.at[grp], pos_buf.at[grp], p_send.at[i], p_recv.at[i], blk, peer)
        for i, peer in enumerate(peers)
    ]
    for copy in pos_copies:
        copy.start()
    for c in range(CHUNKS):
        relay(0, c, key_relay)
    for c in ORDER:
        for d in range(2):
            key_wait(0, d, c)
            key_sends[1, d, c].start()
        if c == max(DETOUR[1]):

            @pl.when(is_relay)
            def _():
                to_par[1].start()

    onward = [
        remote(queries.at[par, r], queries.at[par, r], a_send.at[3 + i], a_recv.at[3 + i], blk, sib)
        for i, r in enumerate(query_rows)
    ]
    to_par[0].wait_recv()
    onward[0].start()
    for c in range(CHUNKS):
        relay(1, c, key_relay)
    to_par[1].wait_recv()
    onward[1].start()
    for copy in pos_copies:
        copy.wait_recv()
    place = jnp.concatenate([pos_buf[t, 0:1, 0:rows] for t in range(GROUPS)], axis=1)
    own_rows = lax.broadcasted_iota(jnp.int32, (rows, block), 0) + grp * rows
    hits = own_rows == place
    hits_buf[...] = jnp.where(hits, 1.0, 0.0).astype(jnp.bfloat16)
    to_sib.wait_recv()
    for copy in onward:
        copy.wait_recv()

    every_query = queries[...].reshape(block, width)

    def score(lo, hi):
        scores[lo:hi, :] = inverse_temp * lax.dot_general(
            keys[lo:hi, :], every_query, (((1,), (1,)), ((), ())), preferred_element_type=jnp.float32
        )
        peak = jnp.max(scores[lo:hi, :], axis=0, keepdims=True)
        return peak, jnp.sum(jnp.exp(scores[lo:hi, :] - peak), axis=0, keepdims=True)

    def merge(stats):
        peak = functools.reduce(jnp.maximum, [p for p, _ in stats])
        return peak, sum(t * jnp.exp(p - peak) for p, t in stats)

    stats = [score(0, near)]
    matched = jnp.sum(jnp.where(hits, scores[0:rows, :], 0.0), axis=0, keepdims=True)
    last = near + (CHUNKS - 1) * 2 * cut
    for c in ORDER:
        if c == ORDER[-1]:
            stats.append(score(near, last))
        for d in range(2):
            key_wait(1, d, c)
    stats.append(score(last, every))
    peak, total = merge(stats)

    stat_buf[grp, 0:1, :] = peak
    stat_buf[grp, 1:2, :] = total
    stat_buf[grp, 2:3, :] = matched
    stat_copies = [
        remote(stat_buf.at[grp], stat_buf.at[grp], s_send.at[i], s_recv.at[i], blk, peer)
        for i, peer in enumerate(peers)
    ]
    for copy in stat_copies:
        copy.start()
    for copy in stat_copies:
        copy.wait_recv()
    peak, total = merge([(stat_buf[t, 0:1, :], stat_buf[t, 1:2, :]) for t in range(GROUPS)])
    lse = peak + jnp.log(total)
    loss_out[...] = lse - sum(stat_buf[t, 2:3, :] for t in range(GROUPS))

    def weigh(lo, hi):
        weights[lo:hi, :] = jnp.exp(scores[lo:hi, :] - lse).astype(jnp.bfloat16)

    def term(lo, hi):
        weigh(lo, hi)
        return jnp.dot(weights[lo:hi, :], every_query, preferred_element_type=jnp.float32)

    code_out, step_out = (code1_out, code2_out), (step1_out, step2_out)
    code_in, step_in = (code1_in, code2_in), (step1_in, step2_in)

    def code_send(hop, d, c):
        part_rows = pl.ds(c * cut, cut)
        by_relay, to_blk = route(hop, d, c)
        slot = pick(by_relay, 2, d)
        return (
            remote(
                code_out[hop].at[d, part_rows], code_in[hop].at[slot, part_rows],
                c_send.at[hop, d, c], c_recv.at[hop, slot, c], to_blk, grp,
            ),
            remote(
                step_out[hop].at[d, c], step_in[hop].at[slot, c],
                t_send.at[hop, d, c], t_recv.at[hop, slot, c], to_blk, grp,
            ),
        )

    def code_wait(hop, d, c):
        codes, steps = code_in[hop].at[d, pl.ds(c * cut, cut)], step_in[hop].at[d, c]
        remote(codes, codes, c_send.at[hop, d, c], c_recv.at[hop, d, c], right, grp).wait_recv()
        remote(steps, steps, t_send.at[hop, d, c], t_recv.at[hop, d, c], right, grp).wait_recv()

    def code_relay(hop, c):
        part_rows = pl.ds(c * cut, cut)
        codes, steps = code_in[hop].at[2, part_rows], step_in[hop].at[2, c]
        return (
            (
                remote(codes, codes, c_send.at[hop, 2, c], c_recv.at[hop, 2, c], relay_to, grp),
                remote(codes, code_in[hop].at[relay_d, part_rows], c_send.at[hop, 2, c], c_recv.at[hop, relay_d, c], relay_to, grp),
            ),
            (
                remote(steps, steps, t_send.at[hop, 2, c], t_recv.at[hop, 2, c], relay_to, grp),
                remote(steps, step_in[hop].at[relay_d, c], t_send.at[hop, 2, c], t_recv.at[hop, relay_d, c], relay_to, grp),
            ),
        )

    code_sends = {(h, d, c): code_send(h, d, c) for h in range(2) for d in range(2) for c in range(CHUNKS)}

    def send_back(hop, d, c, value):
        codes, step = encode(value)
        code_out[hop][d, c * cut : (c + 1) * cut, :] = codes
        step_out[hop][d, c] = step
        for copy in code_sends[hop, d, c]:
            copy.start()

    def received(hop, d, c):
        code_wait(hop, d, c)
        return decode(code_in[hop][d, c * cut : (c + 1) * cut, :], step_in[hop][d, c])

    middle = near + CHUNKS // 2 * 2 * cut
    for parts, lo, hi in (((0, 1), middle, every), ((2, 3), near, middle)):
        far = term(lo, hi)
        for c in parts:
            for d in range(2):
                at = near + (2 * ORDER.index(c) + 1 - d) * cut - lo
                send_back(0, d, c, far[at : at + cut, :])
    weigh(0, near)

    across = (((0,), (0,)), ((), ()))
    pair = GROUPS // 2

    def query_part(chip):
        lanes = pl.ds(pl.multiple_of(chip * pair * rows, 128), pair * rows)
        value = lax.dot_general(weights[:, lanes], keys[0:every, :], across, preferred_element_type=jnp.float32)
        value = value - lax.dot_general(
            hits_buf[:, lanes], keys[0:rows, :], across, preferred_element_type=jnp.float32
        )
        part[pl.ds(chip * pair, pair)] = value.reshape(pair, rows, width)

    chip = grp // pair
    sib_copies = [
        remote(part.at[t], sib_in.at[i], d_send.at[i], d_recv.at[i], blk, sib)
        for i, t in ((0, sib), (1, dia))
    ]
    query_part(1 - chip)
    sib_copies[1].start()
    query_part(chip)
    sib_copies[0].start()
    sib_copies[1].wait_recv()
    x_copies = []
    for i, r in enumerate(query_rows):
        codes, step = encode(part[par, r] + sib_in[1, r])
        codex_out[r, :] = codes
        stepx_out[i] = step
        x_copies.append((
            remote(codex_out.at[r], codex_in.at[r], x_send.at[0, i], x_recv.at[0, i], blk, par),
            remote(stepx_out.at[i], stepx_in.at[i], x_send.at[1, i], x_recv.at[1, i], blk, par),
        ))
    for copy in x_copies[0]:
        copy.start()

    for c in range(CHUNKS):
        relay(0, c, code_relay)
    home[...] = jnp.dot(weights[0:near, :], every_query, preferred_element_type=jnp.float32)
    home[0:rows, :] -= jnp.dot(hits_buf[...], every_query, preferred_element_type=jnp.float32)
    for c in ORDER:
        for d in range(2):
            lo = rows * (2 - d) + c * cut
            send_back(1, d, c, home[lo : lo + cut, :] + received(0, d, c))
        if c == max(DETOUR[1]):
            for copy in x_copies[1]:
                copy.start()

    for c in range(CHUNKS):
        relay(1, c, code_relay)
    for c in ORDER:
        lo = c * cut
        grad_b_out[lo : lo + cut, :] = inverse_temp * (
            home[lo : lo + cut, :] + received(1, 0, c) + received(1, 1, c)
        )
        if c == ORDER[1]:
            sib_copies[0].wait_recv()
            for i, r in enumerate(query_rows):
                for copy in x_copies[i]:
                    copy.wait_recv()
                grad_a_out[r, :] = inverse_temp * (
                    part[grp, r] + sib_in[0, r] + decode(codex_in[r, :], stepx_in[i])
                )

    for copy in key_sends.values():
        copy.wait_send()
    for pair in code_sends.values():
        for copy in pair:
            copy.wait_send()
    for copy in (*to_par, to_sib, *onward, *pos_copies, *stat_copies, *sib_copies, *x_copies[0], *x_copies[1]):
        copy.wait_send()

    @pl.when(is_relay)
    def _():
        for hop in range(2):
            for c in DETOUR[hop]:
                for _, leaving in (*key_relay(hop, c), *code_relay(hop, c)):
                    leaving.wait_send()


def body(view_a, view_b, positive):
    rows, width = view_a.shape
    block = rows * GROUPS
    lanes = -(-rows // 128) * 128
    vmem = pl.BlockSpec(memory_space=pltpu.VMEM)
    hbm = pl.BlockSpec(memory_space=pl.ANY)
    dma = pltpu.SemaphoreType.DMA
    f32, bf16, i16 = jnp.float32, jnp.bfloat16, jnp.int16
    codes_out, steps_out = pltpu.VMEM((2, rows, width), i16), pltpu.VMEM((2, CHUNKS, 1, width), f32)
    codes_in, steps_in = pltpu.VMEM((3, rows, width), i16), pltpu.VMEM((3, CHUNKS, 1, width), f32)
    loss, grad_a, grad_b = pl.pallas_call(
        kernel,
        out_shape=(
            jax.ShapeDtypeStruct((1, block), f32),
            jax.ShapeDtypeStruct((rows, width), f32),
            jax.ShapeDtypeStruct((rows, width), f32),
        ),
        in_specs=[hbm, hbm, vmem],
        out_specs=(vmem, vmem, vmem),
        scratch_shapes=[
            pltpu.VMEM((GROUPS, rows, width), bf16),
            pltpu.VMEM(((WINDOW + 2) * rows, width), bf16),
            pltpu.VMEM((GROUPS, 8, lanes), jnp.int32),
            pltpu.VMEM((GROUPS, 8, block), f32),
            pltpu.VMEM((WINDOW * rows, block), f32),
            pltpu.VMEM((WINDOW * rows, block), bf16),
            pltpu.VMEM((rows, block), bf16),
            pltpu.VMEM(((SPAN + 1) * rows, width), f32),
            codes_out, steps_out, codes_in, steps_in, codes_out, steps_out, codes_in, steps_in,
            pltpu.VMEM((GROUPS, rows, width), f32),
            pltpu.VMEM((2, rows, width), f32),
            pltpu.VMEM((rows, width), i16),
            pltpu.VMEM((2, 1, width), f32),
            pltpu.VMEM((rows, width), i16),
            pltpu.VMEM((2, 1, width), f32),
            dma((2,)),
            dma((2, 3, CHUNKS)), dma((2, 3, CHUNKS)),
            dma((5,)), dma((5,)),
            dma((3,)), dma((3,)),
            dma((3,)), dma((3,)),
            dma((2, 3, CHUNKS)), dma((2, 3, CHUNKS)),
            dma((2, 3, CHUNKS)), dma((2, 3, CHUNKS)),
            dma((2,)), dma((2,)),
            dma((2, 2)), dma((2, 2)),
        ],
        compiler_params=pltpu.CompilerParams(
            collective_id=0, has_side_effects=True, vmem_limit_bytes=56 * 2**20
        ),
        cost_estimate=pl.CostEstimate(
            flops=2 * block * rows * width * 17, bytes_accessed=rows * width * 12,
            transcendentals=2 * WINDOW * rows * block,
        ),
    )(view_a, view_b, positive.reshape(1, rows))
    row_loss = lax.dynamic_slice_in_dim(loss[0], lax.axis_index("grp") * rows, rows, 0)
    return row_loss, grad_a, grad_b


def solution(mesh):
    in_specs = (P(("blk", "grp"), None), P(("blk", "grp"), None), P(("blk", "grp")))
    out_specs = (P(("blk", "grp")), P(("blk", "grp"), None), P(("blk", "grp"), None))
    return jax.shard_map(body, mesh=mesh, in_specs=in_specs, out_specs=out_specs, check_vma=False)
```

```python
import functools

import jax
import jax.numpy as jnp
from jax import lax
from jax.experimental import pallas as pl
from jax.experimental.pallas import tpu as pltpu
from jax.sharding import PartitionSpec as P

SPAN = 2
WINDOW = 2 * SPAN + 1
GROUPS = 4
CHUNKS = 4
DETOUR = ((0, 1), (2, 3))
ORDER = (2, 3, 0, 1)
inverse_temp = 20.0
MESH = pl.DeviceIdType.MESH
TOP = 32766.0


def encode(x):
    peak = jnp.max(jnp.abs(x), axis=0, keepdims=True)
    alive = peak > 1e-30
    scale = jnp.where(alive, TOP / jnp.where(alive, peak, 1.0), 0.0)
    codes = jnp.round(x * scale).astype(jnp.int32).astype(jnp.int16)
    return codes, jnp.where(alive, peak * (1.0 / TOP), 0.0)


def decode(codes, step):
    return codes.astype(jnp.int32).astype(jnp.float32) * step


def kernel(
    a_in, b_in, pos_in, loss_out, grad_a_out, grad_b_out,
    queries, keys, pos_buf, stat_buf, scores, weights, hits_buf, home,
    code1_out, step1_out, code1_in, step1_in, code2_out, step2_out, code2_in, step2_in,
    part, sib_in, codex_out, stepx_out, codex_in, stepx_in,
    load_sem, b_send, b_recv, a_send, a_recv, p_send, p_recv, s_send, s_recv,
    c_send, c_recv, t_send, t_recv, d_send, d_recv, x_send, x_recv,
):
    rows, width = a_in.shape
    block = rows * GROUPS
    cut = rows // CHUNKS
    near = (SPAN + 1) * rows
    every = WINDOW * rows
    blk = lax.axis_index("blk")
    grp = lax.axis_index("grp")
    blocks = lax.axis_size("blk")
    right = lax.rem(blk + 1, blocks)
    left = lax.rem(blk + blocks - 1, blocks)
    sib = grp + 1 - 2 * lax.rem(grp, 2)
    par = lax.rem(grp + 2, GROUPS)
    dia = lax.rem(sib + 2, GROUPS)
    peers = (sib, par, dia)

    half = blocks // 2
    spot = lax.rem(blk, half)
    is_last, is_first = spot == half - 1, spot == 0
    is_relay = jnp.logical_or(is_last, is_first)
    detour = (is_last, is_first)
    across_x = lax.rem(blk + half, blocks)
    relay_to = lax.rem(blk + jnp.where(is_last, half + 1, half - 1), blocks)
    relay_d = jnp.where(is_last, 0, 1)

    def route(hop, d, c):
        if c not in DETOUR[hop]:
            return False, (right, left)[d]
        return detour[d], jnp.where(detour[d], across_x, (right, left)[d])

    def pick(flag, a, b):
        return b if flag is False else jnp.where(flag, a, b)

    def remote(src, dst, send, recv, to_blk, to_grp):
        return pltpu.make_async_remote_copy(
            src_ref=src, dst_ref=dst, send_sem=send, recv_sem=recv,
            device_id=(to_blk, to_grp), device_id_type=MESH,
        )

    def span(lo, size):
        return pl.ds(pl.multiple_of(lo, 16), size)

    load_b = pltpu.make_async_copy(b_in, keys.at[pl.ds(0, rows)], load_sem.at[0])
    load_a = pltpu.make_async_copy(a_in, queries.at[grp], load_sem.at[1])
    load_b.start()
    load_a.start()

    barrier = pltpu.get_barrier_semaphore()

    def greet(to_blk, to_grp):
        pl.semaphore_signal(barrier, inc=1, device_id=(to_blk, to_grp), device_id_type=MESH)

    greet(right, grp)
    greet(left, grp)
    for peer in peers:
        greet(blk, peer)

    @pl.when(is_relay)
    def _():
        greet(across_x, grp)
        greet(relay_to, grp)

    pos_buf[grp] = jnp.zeros(pos_buf.shape[1:], jnp.int32)
    pos_buf[grp, 0:1, 0:rows] = pos_in[...] - blk * block
    pl.semaphore_wait(barrier, 5 + jnp.where(is_relay, 2, 0))
    load_b.wait()

    def key_place(hop, d, c):
        if hop == 0:
            lands = rows * (1 + d) + c * cut
        else:
            lands = near + (2 * ORDER.index(c) + d) * cut
        return lands, every + hop * rows + c * cut

    def key_send(hop, d, c):
        src = c * cut if hop == 0 else rows * (1 + d) + c * cut
        direct, held = key_place(hop, d, c)
        by_relay, to_blk = route(hop, d, c)
        return remote(
            keys.at[pl.ds(src, cut)], keys.at[span(pick(by_relay, held, direct), cut)],
            b_send.at[hop, d, c], b_recv.at[hop, pick(by_relay, 2, d), c], to_blk, grp,
        )

    def key_wait(hop, d, c):
        place = keys.at[pl.ds(key_place(hop, d, c)[0], cut)]
        remote(place, place, b_send.at[hop, d, c], b_recv.at[hop, d, c], right, grp).wait_recv()

    def key_relay(hop, c):
        held = keys.at[pl.ds(key_place(hop, 0, c)[1], cut)]
        lands = jnp.where(is_last, key_place(hop, 0, c)[0], key_place(hop, 1, c)[0])
        return ((
            remote(held, held, b_send.at[hop, 2, c], b_recv.at[hop, 2, c], relay_to, grp),
            remote(held, keys.at[span(lands, cut)], b_send.at[hop, 2, c], b_recv.at[hop, relay_d, c], relay_to, grp),
        ),)

    def relay(hop, c, copies):
        if c not in DETOUR[hop]:
            return

        @pl.when(is_relay)
        def _():
            for arriving, _ in copies(hop, c):
                arriving.wait_recv()
            for _, leaving in copies(hop, c):
                leaving.start()

    key_sends = {(h, d, c): key_send(h, d, c) for h in range(2) for d in range(2) for c in range(CHUNKS)}
    middle_row = rows // 2
    query_rows = [pl.ds(i * middle_row, middle_row) for i in range(2)]
    to_par = [
        remote(queries.at[grp, r], queries.at[grp, r], a_send.at[1 + i], a_recv.at[1 + i], blk, par)
        for i, r in enumerate(query_rows)
    ]
    to_sib = remote(queries.at[grp], queries.at[grp], a_send.at[0], a_recv.at[0], blk, sib)
    for c in range(CHUNKS):
        for d in range(2):
            key_sends[0, d, c].start()
    load_a.wait()
    to_par[0].start()
    to_sib.start()

    @pl.when(jnp.logical_not(is_relay))
    def _():
        to_par[1].start()

    pos_copies = [
        remote(pos_buf.at[grp], pos_buf.at[grp], p_send.at[i], p_recv.at[i], blk, peer)
        for i, peer in enumerate(peers)
    ]
    for copy in pos_copies:
        copy.start()
    for c in range(CHUNKS):
        relay(0, c, key_relay)
    for c in ORDER:
        for d in range(2):
            key_wait(0, d, c)
            key_sends[1, d, c].start()
        if c == max(DETOUR[1]):

            @pl.when(is_relay)
            def _():
                to_par[1].start()

    onward = [
        remote(queries.at[par, r], queries.at[par, r], a_send.at[3 + i], a_recv.at[3 + i], blk, sib)
        for i, r in enumerate(query_rows)
    ]
    to_par[0].wait_recv()
    onward[0].start()
    for c in range(CHUNKS):
        relay(1, c, key_relay)
    to_par[1].wait_recv()
    onward[1].start()
    for copy in pos_copies:
        copy.wait_recv()
    place = jnp.concatenate([pos_buf[t, 0:1, 0:rows] for t in range(GROUPS)], axis=1)
    own_rows = lax.broadcasted_iota(jnp.int32, (rows, block), 0) + grp * rows
    hits = own_rows == place
    hits_buf[...] = jnp.where(hits, 1.0, 0.0).astype(jnp.bfloat16)
    to_sib.wait_recv()
    for copy in onward:
        copy.wait_recv()

    every_query = queries[...].reshape(block, width)

    def score(lo, hi):
        scores[lo:hi, :] = inverse_temp * lax.dot_general(
            keys[lo:hi, :], every_query, (((1,), (1,)), ((), ())), preferred_element_type=jnp.float32
        )
        peak = jnp.max(scores[lo:hi, :], axis=0, keepdims=True)
        return peak, jnp.sum(jnp.exp(scores[lo:hi, :] - peak), axis=0, keepdims=True)

    def merge(stats):
        peak = functools.reduce(jnp.maximum, [p for p, _ in stats])
        return peak, sum(t * jnp.exp(p - peak) for p, t in stats)

    stats = [score(0, near)]
    matched = jnp.sum(jnp.where(hits, scores[0:rows, :], 0.0), axis=0, keepdims=True)
    last = near + (CHUNKS - 1) * 2 * cut
    for c in ORDER:
        if c == ORDER[-1]:
            stats.append(score(near, last))
        for d in range(2):
            key_wait(1, d, c)
    stats.append(score(last, every))
    peak, total = merge(stats)

    stat_buf[grp, 0:1, :] = peak
    stat_buf[grp, 1:2, :] = total
    stat_buf[grp, 2:3, :] = matched
    stat_copies = [
        remote(stat_buf.at[grp], stat_buf.at[grp], s_send.at[i], s_recv.at[i], blk, peer)
        for i, peer in enumerate(peers)
    ]
    for copy in stat_copies:
        copy.start()
    for copy in stat_copies:
        copy.wait_recv()
    peak, total = merge([(stat_buf[t, 0:1, :], stat_buf[t, 1:2, :]) for t in range(GROUPS)])
    lse = peak + jnp.log(total)
    losses = lse - sum(stat_buf[t, 2:3, :] for t in range(GROUPS))
    own_loss = losses[:, 0:rows]
    for t in range(1, GROUPS):
        own_loss = jnp.where(grp == t, losses[:, t * rows : (t + 1) * rows], own_loss)
    loss_out[...] = own_loss

    def weigh(lo, hi):
        weights[lo:hi, :] = jnp.exp(scores[lo:hi, :] - lse).astype(jnp.bfloat16)

    def term(lo, hi):
        weigh(lo, hi)
        return jnp.dot(weights[lo:hi, :], every_query, preferred_element_type=jnp.float32)

    code_out, step_out = (code1_out, code2_out), (step1_out, step2_out)
    code_in, step_in = (code1_in, code2_in), (step1_in, step2_in)

    def code_send(hop, d, c):
        part_rows = pl.ds(c * cut, cut)
        by_relay, to_blk = route(hop, d, c)
        slot = pick(by_relay, 2, d)
        return (
            remote(
                code_out[hop].at[d, part_rows], code_in[hop].at[slot, part_rows],
                c_send.at[hop, d, c], c_recv.at[hop, slot, c], to_blk, grp,
            ),
            remote(
                step_out[hop].at[d, c], step_in[hop].at[slot, c],
                t_send.at[hop, d, c], t_recv.at[hop, slot, c], to_blk, grp,
            ),
        )

    def code_wait(hop, d, c):
        codes, steps = code_in[hop].at[d, pl.ds(c * cut, cut)], step_in[hop].at[d, c]
        remote(codes, codes, c_send.at[hop, d, c], c_recv.at[hop, d, c], right, grp).wait_recv()
        remote(steps, steps, t_send.at[hop, d, c], t_recv.at[hop, d, c], right, grp).wait_recv()

    def code_relay(hop, c):
        part_rows = pl.ds(c * cut, cut)
        codes, steps = code_in[hop].at[2, part_rows], step_in[hop].at[2, c]
        return (
            (
                remote(codes, codes, c_send.at[hop, 2, c], c_recv.at[hop, 2, c], relay_to, grp),
                remote(codes, code_in[hop].at[relay_d, part_rows], c_send.at[hop, 2, c], c_recv.at[hop, relay_d, c], relay_to, grp),
            ),
            (
                remote(steps, steps, t_send.at[hop, 2, c], t_recv.at[hop, 2, c], relay_to, grp),
                remote(steps, step_in[hop].at[relay_d, c], t_send.at[hop, 2, c], t_recv.at[hop, relay_d, c], relay_to, grp),
            ),
        )

    code_sends = {(h, d, c): code_send(h, d, c) for h in range(2) for d in range(2) for c in range(CHUNKS)}

    def send_back(hop, d, c, value):
        codes, step = encode(value)
        code_out[hop][d, c * cut : (c + 1) * cut, :] = codes
        step_out[hop][d, c] = step
        for copy in code_sends[hop, d, c]:
            copy.start()

    def received(hop, d, c):
        code_wait(hop, d, c)
        return decode(code_in[hop][d, c * cut : (c + 1) * cut, :], step_in[hop][d, c])

    middle = near + CHUNKS // 2 * 2 * cut
    for parts, lo, hi in (((0, 1), middle, every), ((2, 3), near, middle)):
        far = term(lo, hi)
        for c in parts:
            for d in range(2):
                at = near + (2 * ORDER.index(c) + 1 - d) * cut - lo
                send_back(0, d, c, far[at : at + cut, :])
    weigh(0, near)

    across = (((0,), (0,)), ((), ()))
    pair = GROUPS // 2

    def query_part(chip):
        lanes = pl.ds(pl.multiple_of(chip * pair * rows, 128), pair * rows)
        value = lax.dot_general(weights[:, lanes], keys[0:every, :], across, preferred_element_type=jnp.float32)
        value = value - lax.dot_general(
            hits_buf[:, lanes], keys[0:rows, :], across, preferred_element_type=jnp.float32
        )
        part[pl.ds(chip * pair, pair)] = value.reshape(pair, rows, width)

    chip = grp // pair
    sib_copies = [
        remote(part.at[t], sib_in.at[i], d_send.at[i], d_recv.at[i], blk, sib)
        for i, t in ((0, sib), (1, dia))
    ]
    query_part(1 - chip)
    sib_copies[1].start()
    query_part(chip)
    sib_copies[0].start()
    sib_copies[1].wait_recv()
    x_copies = []
    for i, r in enumerate(query_rows):
        codes, step = encode(part[par, r] + sib_in[1, r])
        codex_out[r, :] = codes
        stepx_out[i] = step
        x_copies.append((
            remote(codex_out.at[r], codex_in.at[r], x_send.at[0, i], x_recv.at[0, i], blk, par),
            remote(stepx_out.at[i], stepx_in.at[i], x_send.at[1, i], x_recv.at[1, i], blk, par),
        ))
    for copy in x_copies[0]:
        copy.start()

    @pl.when(jnp.logical_not(is_relay))
    def _():
        for copy in x_copies[1]:
            copy.start()

    for c in range(CHUNKS):
        relay(0, c, code_relay)
    home[...] = jnp.dot(weights[0:near, :], every_query, preferred_element_type=jnp.float32)
    home[0:rows, :] -= jnp.dot(hits_buf[...], every_query, preferred_element_type=jnp.float32)
    for c in ORDER:
        for d in range(2):
            lo = rows * (2 - d) + c * cut
            send_back(1, d, c, home[lo : lo + cut, :] + received(0, d, c))
        if c == max(DETOUR[1]):

            @pl.when(is_relay)
            def _():
                for copy in x_copies[1]:
                    copy.start()

    for c in range(CHUNKS):
        relay(1, c, code_relay)
    for c in ORDER:
        lo = c * cut
        grad_b_out[lo : lo + cut, :] = home[lo : lo + cut, :] + received(1, 0, c) + received(1, 1, c)
        if c == ORDER[1]:
            sib_copies[0].wait_recv()
            for i, r in enumerate(query_rows):
                for copy in x_copies[i]:
                    copy.wait_recv()
                grad_a_out[r, :] = part[grp, r] + sib_in[0, r] + decode(codex_in[r, :], stepx_in[i])

    for copy in key_sends.values():
        copy.wait_send()
    for pair in code_sends.values():
        for copy in pair:
            copy.wait_send()
    for copy in (*to_par, to_sib, *onward, *pos_copies, *stat_copies, *sib_copies, *x_copies[0], *x_copies[1]):
        copy.wait_send()

    @pl.when(is_relay)
    def _():
        for hop in range(2):
            for c in DETOUR[hop]:
                for _, leaving in (*key_relay(hop, c), *code_relay(hop, c)):
                    leaving.wait_send()


def body(view_a, view_b, positive):
    rows, width = view_a.shape
    block = rows * GROUPS
    lanes = -(-rows // 128) * 128
    vmem = pl.BlockSpec(memory_space=pltpu.VMEM)
    hbm = pl.BlockSpec(memory_space=pl.ANY)
    dma = pltpu.SemaphoreType.DMA
    f32, bf16, i16 = jnp.float32, jnp.bfloat16, jnp.int16
    codes_out, steps_out = pltpu.VMEM((2, rows, width), i16), pltpu.VMEM((2, CHUNKS, 1, width), f32)
    codes_in, steps_in = pltpu.VMEM((3, rows, width), i16), pltpu.VMEM((3, CHUNKS, 1, width), f32)
    loss, grad_a, grad_b = pl.pallas_call(
        kernel,
        out_shape=(
            pltpu.VMEM((1, rows), f32),
            pltpu.VMEM((rows, width), f32),
            pltpu.VMEM((rows, width), f32),
        ),
        in_specs=[hbm, hbm, vmem],
        out_specs=(vmem, vmem, vmem),
        scratch_shapes=[
            pltpu.VMEM((GROUPS, rows, width), bf16),
            pltpu.VMEM(((WINDOW + 2) * rows, width), bf16),
            pltpu.VMEM((GROUPS, 8, lanes), jnp.int32),
            pltpu.VMEM((GROUPS, 8, block), f32),
            pltpu.VMEM((WINDOW * rows, block), f32),
            pltpu.VMEM((WINDOW * rows, block), bf16),
            pltpu.VMEM((rows, block), bf16),
            pltpu.VMEM(((SPAN + 1) * rows, width), f32),
            codes_out, steps_out, codes_in, steps_in, codes_out, steps_out, codes_in, steps_in,
            pltpu.VMEM((GROUPS, rows, width), f32),
            pltpu.VMEM((2, rows, width), f32),
            pltpu.VMEM((rows, width), i16),
            pltpu.VMEM((2, 1, width), f32),
            pltpu.VMEM((rows, width), i16),
            pltpu.VMEM((2, 1, width), f32),
            dma((2,)),
            dma((2, 3, CHUNKS)), dma((2, 3, CHUNKS)),
            dma((5,)), dma((5,)),
            dma((3,)), dma((3,)),
            dma((3,)), dma((3,)),
            dma((2, 3, CHUNKS)), dma((2, 3, CHUNKS)),
            dma((2, 3, CHUNKS)), dma((2, 3, CHUNKS)),
            dma((2,)), dma((2,)),
            dma((2, 2)), dma((2, 2)),
        ],
        compiler_params=pltpu.CompilerParams(
            collective_id=0, has_side_effects=True, vmem_limit_bytes=53 * 2**20
        ),
        cost_estimate=pl.CostEstimate(
            flops=2 * block * rows * width * 17, bytes_accessed=rows * width * 12,
            transcendentals=2 * WINDOW * rows * block,
        ),
    )(view_a, view_b, positive.reshape(1, rows))
    return loss.reshape(rows), inverse_temp * grad_a, inverse_temp * grad_b


def solution(mesh):
    in_specs = (P(("blk", "grp"), None), P(("blk", "grp"), None), P(("blk", "grp")))
    out_specs = (P(("blk", "grp")), P(("blk", "grp"), None), P(("blk", "grp"), None))
    return jax.shard_map(body, mesh=mesh, in_specs=in_specs, out_specs=out_specs, check_vma=False)
```

```python
import functools

import jax
import jax.numpy as jnp
from jax import lax
from jax.experimental import pallas as pl
from jax.experimental.pallas import tpu as pltpu
from jax.sharding import PartitionSpec as P

SPAN = 2
WINDOW = 2 * SPAN + 1
GROUPS = 4
CHUNKS = 4
KEY_DETOUR = ((0, 1), (0,))
CODE_DETOUR = ((0,), (0, 1))
inverse_temp = 20.0
MESH = pl.DeviceIdType.MESH
TOP = 32766.0


def encode(x):
    peak = jnp.max(jnp.abs(x), axis=0, keepdims=True)
    alive = peak > 1e-30
    scale = jnp.where(alive, TOP / jnp.where(alive, peak, 1.0), 0.0)
    codes = jnp.round(x * scale).astype(jnp.int32).astype(jnp.int16)
    return codes, jnp.where(alive, peak * (1.0 / TOP), 0.0)


def decode(codes, step):
    return codes.astype(jnp.int32).astype(jnp.float32) * step


def kernel(
    a_in, b_in, pos_in, loss_out, grad_a_out, grad_b_out,
    queries, keys, pos_buf, stat_buf, scores, weights, hits_buf, home,
    code1_out, step1_out, code1_in, step1_in, code2_out, step2_out, code2_in, step2_in,
    part, sib_in, codex_out, stepx_out, codex_in, stepx_in,
    load_sem, b_send, b_recv, a_send, a_recv, p_send, p_recv, s_send, s_recv,
    c_send, c_recv, t_send, t_recv, d_send, d_recv, x_send, x_recv,
):
    rows, width = a_in.shape
    block = rows * GROUPS
    cut = rows // CHUNKS
    near = (SPAN + 1) * rows
    every = WINDOW * rows
    blk = lax.axis_index("blk")
    grp = lax.axis_index("grp")
    blocks = lax.axis_size("blk")
    right = lax.rem(blk + 1, blocks)
    left = lax.rem(blk + blocks - 1, blocks)
    sib = grp + 1 - 2 * lax.rem(grp, 2)
    par = lax.rem(grp + 2, GROUPS)
    dia = lax.rem(sib + 2, GROUPS)
    peers = (sib, par, dia)

    half = blocks // 2
    spot = lax.rem(blk, half)
    is_last, is_first = spot == half - 1, spot == 0
    is_relay = jnp.logical_or(is_last, is_first)
    detour = (is_last, is_first)
    across_x = lax.rem(blk + half, blocks)
    relay_to = lax.rem(blk + jnp.where(is_last, half + 1, half - 1), blocks)
    relay_d = jnp.where(is_last, 0, 1)

    def route(detours, d, c):
        if c not in detours:
            return False, (right, left)[d]
        return detour[d], jnp.where(detour[d], across_x, (right, left)[d])

    def pick(flag, a, b):
        return b if flag is False else jnp.where(flag, a, b)

    def remote(src, dst, send, recv, to_blk, to_grp):
        return pltpu.make_async_remote_copy(
            src_ref=src, dst_ref=dst, send_sem=send, recv_sem=recv,
            device_id=(to_blk, to_grp), device_id_type=MESH,
        )

    def span(lo, size):
        return pl.ds(pl.multiple_of(lo, 16), size)

    load_b = pltpu.make_async_copy(b_in, keys.at[pl.ds(0, rows)], load_sem.at[0])
    load_a = pltpu.make_async_copy(a_in, queries.at[grp], load_sem.at[1])
    load_b.start()
    load_a.start()

    barrier = pltpu.get_barrier_semaphore()

    def greet(to_blk, to_grp):
        pl.semaphore_signal(barrier, inc=1, device_id=(to_blk, to_grp), device_id_type=MESH)

    greet(right, grp)
    greet(left, grp)
    for peer in peers:
        greet(blk, peer)

    @pl.when(is_relay)
    def _():
        greet(across_x, grp)
        greet(relay_to, grp)

    pos_buf[grp] = jnp.zeros(pos_buf.shape[1:], jnp.int32)
    pos_buf[grp, 0:1, 0:rows] = pos_in[...] - blk * block
    pl.semaphore_wait(barrier, 5 + jnp.where(is_relay, 2, 0))
    load_b.wait()

    def key_place(hop, d, c):
        if hop == 0:
            lands = rows * (1 + d) + c * cut
        else:
            lands = near + (2 * c + d) * cut
        return lands, every + hop * rows + c * cut

    def key_send(hop, d, c):
        src = c * cut if hop == 0 else rows * (1 + d) + c * cut
        direct, held = key_place(hop, d, c)
        by_relay, to_blk = route(KEY_DETOUR[hop], d, c)
        return remote(
            keys.at[pl.ds(src, cut)], keys.at[span(pick(by_relay, held, direct), cut)],
            b_send.at[hop, d, c], b_recv.at[hop, pick(by_relay, 2, d), c], to_blk, grp,
        )

    def key_wait(hop, d, c):
        place = keys.at[pl.ds(key_place(hop, d, c)[0], cut)]
        remote(place, place, b_send.at[hop, d, c], b_recv.at[hop, d, c], right, grp).wait_recv()

    def key_relay(hop, c):
        held = keys.at[pl.ds(key_place(hop, 0, c)[1], cut)]
        lands = jnp.where(is_last, key_place(hop, 0, c)[0], key_place(hop, 1, c)[0])
        return ((
            remote(held, held, b_send.at[hop, 2, c], b_recv.at[hop, 2, c], relay_to, grp),
            remote(held, keys.at[span(lands, cut)], b_send.at[hop, 2, c], b_recv.at[hop, relay_d, c], relay_to, grp),
        ),)

    def relay(hop, c, copies):
        @pl.when(is_relay)
        def _():
            for arriving, _ in copies(hop, c):
                arriving.wait_recv()
            for _, leaving in copies(hop, c):
                leaving.start()

    key_sends = {(h, d, c): key_send(h, d, c) for h in range(2) for d in range(2) for c in range(CHUNKS)}
    middle_row = rows // 2
    query_rows = [pl.ds(i * middle_row, middle_row) for i in range(2)]
    to_par = [
        remote(queries.at[grp, r], queries.at[grp, r], a_send.at[1 + i], a_recv.at[1 + i], blk, par)
        for i, r in enumerate(query_rows)
    ]
    to_sib = remote(queries.at[grp], queries.at[grp], a_send.at[0], a_recv.at[0], blk, sib)
    for c in range(CHUNKS):
        for d in range(2):
            key_sends[0, d, c].start()
    load_a.wait()
    to_sib.start()

    @pl.when(jnp.logical_not(is_relay))
    def _():
        for copy in to_par:
            copy.start()

    pos_copies = [
        remote(pos_buf.at[grp], pos_buf.at[grp], p_send.at[i], p_recv.at[i], blk, peer)
        for i, peer in enumerate(peers)
    ]
    for copy in pos_copies:
        copy.start()

    def take(d, c):
        key_wait(0, d, c)
        key_sends[1, d, c].start()

    def take_at_edge(inner):
        for c in KEY_DETOUR[0]:
            take(inner, c)
            for arriving, leaving in key_relay(0, c):
                arriving.wait_recv()
                leaving.start()
        for copy in to_par:
            copy.start()
        direct = [c for c in range(CHUNKS) if c not in KEY_DETOUR[0]]
        for d, parts in ((inner, direct), (1 - inner, direct), (1 - inner, KEY_DETOUR[0])):
            for c in parts:
                take(d, c)
        for c in KEY_DETOUR[1]:
            for arriving, leaving in key_relay(1, c):
                arriving.wait_recv()
                leaving.start()

    @pl.when(is_last)
    def _():
        take_at_edge(0)

    @pl.when(is_first)
    def _():
        take_at_edge(1)

    @pl.when(jnp.logical_not(is_relay))
    def _():
        for c in range(CHUNKS):
            for d in range(2):
                take(d, c)

    onward = [
        remote(queries.at[par, r], queries.at[par, r], a_send.at[3 + i], a_recv.at[3 + i], blk, sib)
        for i, r in enumerate(query_rows)
    ]
    for copy in pos_copies:
        copy.wait_recv()
    place = jnp.concatenate([pos_buf[t, 0:1, 0:rows] for t in range(GROUPS)], axis=1)
    own_rows = lax.broadcasted_iota(jnp.int32, (rows, block), 0) + grp * rows
    hits = own_rows == place
    hits_buf[...] = jnp.where(hits, 1.0, 0.0).astype(jnp.bfloat16)
    pair = GROUPS // 2
    chip = grp // pair

    def lanes_of(chip):
        return pl.ds(pl.multiple_of(chip * pair * rows, 128), pair * rows)

    def score_near(chip):
        lanes = lanes_of(chip)
        value = inverse_temp * lax.dot_general(
            keys[0:near, :], queries[pl.ds(chip * pair, pair)].reshape(pair * rows, width),
            (((1,), (1,)), ((), ())), preferred_element_type=jnp.float32,
        )
        scores[0:near, lanes] = value
        peak = jnp.max(value, axis=0, keepdims=True)
        stat_buf[grp, 3:4, lanes] = peak
        stat_buf[grp, 4:5, lanes] = jnp.sum(jnp.exp(value - peak), axis=0, keepdims=True)

    to_sib.wait_recv()
    score_near(chip)
    for i in range(2):
        to_par[i].wait_recv()
        onward[i].start()
    for copy in onward:
        copy.wait_recv()
    score_near(1 - chip)

    every_query = queries[...].reshape(block, width)

    def score(lo, hi):
        scores[lo:hi, :] = inverse_temp * lax.dot_general(
            keys[lo:hi, :], every_query, (((1,), (1,)), ((), ())), preferred_element_type=jnp.float32
        )
        peak = jnp.max(scores[lo:hi, :], axis=0, keepdims=True)
        return peak, jnp.sum(jnp.exp(scores[lo:hi, :] - peak), axis=0, keepdims=True)

    def merge(stats):
        peak = functools.reduce(jnp.maximum, [p for p, _ in stats])
        return peak, sum(t * jnp.exp(p - peak) for p, t in stats)

    stats = [(stat_buf[grp, 3:4, :], stat_buf[grp, 4:5, :])]
    matched = jnp.sum(jnp.where(hits, scores[0:rows, :], 0.0), axis=0, keepdims=True)
    last = near + (CHUNKS - 1) * 2 * cut
    for c in range(CHUNKS):
        if c == CHUNKS - 1:
            stats.append(score(near, last))
        for d in range(2):
            key_wait(1, d, c)
    stats.append(score(last, every))
    peak, total = merge(stats)

    stat_buf[grp, 0:1, :] = peak
    stat_buf[grp, 1:2, :] = total
    stat_buf[grp, 2:3, :] = matched
    stat_copies = [
        remote(stat_buf.at[grp], stat_buf.at[grp], s_send.at[i], s_recv.at[i], blk, peer)
        for i, peer in enumerate(peers)
    ]
    for copy in stat_copies:
        copy.start()
    for copy in stat_copies:
        copy.wait_recv()
    peak, total = merge([(stat_buf[t, 0:1, :], stat_buf[t, 1:2, :]) for t in range(GROUPS)])
    lse = peak + jnp.log(total)
    losses = lse - sum(stat_buf[t, 2:3, :] for t in range(GROUPS))
    own_loss = losses[:, 0:rows]
    for t in range(1, GROUPS):
        own_loss = jnp.where(grp == t, losses[:, t * rows : (t + 1) * rows], own_loss)
    loss_out[...] = own_loss

    def weigh(lo, hi):
        weights[lo:hi, :] = jnp.exp(scores[lo:hi, :] - lse).astype(jnp.bfloat16)

    def term(lo, hi):
        weigh(lo, hi)
        return jnp.dot(weights[lo:hi, :], every_query, preferred_element_type=jnp.float32)

    code_out, step_out = (code1_out, code2_out), (step1_out, step2_out)
    code_in, step_in = (code1_in, code2_in), (step1_in, step2_in)

    def code_send(hop, d, c):
        part_rows = pl.ds(c * cut, cut)
        by_relay, to_blk = route(CODE_DETOUR[hop], d, c)
        slot = pick(by_relay, 2, d)
        return (
            remote(
                code_out[hop].at[d, part_rows], code_in[hop].at[slot, part_rows],
                c_send.at[hop, d, c], c_recv.at[hop, slot, c], to_blk, grp,
            ),
            remote(
                step_out[hop].at[d, c], step_in[hop].at[slot, c],
                t_send.at[hop, d, c], t_recv.at[hop, slot, c], to_blk, grp,
            ),
        )

    def code_wait(hop, d, c):
        codes, steps = code_in[hop].at[d, pl.ds(c * cut, cut)], step_in[hop].at[d, c]
        remote(codes, codes, c_send.at[hop, d, c], c_recv.at[hop, d, c], right, grp).wait_recv()
        remote(steps, steps, t_send.at[hop, d, c], t_recv.at[hop, d, c], right, grp).wait_recv()

    def code_relay(hop, c):
        part_rows = pl.ds(c * cut, cut)
        codes, steps = code_in[hop].at[2, part_rows], step_in[hop].at[2, c]
        return (
            (
                remote(codes, codes, c_send.at[hop, 2, c], c_recv.at[hop, 2, c], relay_to, grp),
                remote(codes, code_in[hop].at[relay_d, part_rows], c_send.at[hop, 2, c], c_recv.at[hop, relay_d, c], relay_to, grp),
            ),
            (
                remote(steps, steps, t_send.at[hop, 2, c], t_recv.at[hop, 2, c], relay_to, grp),
                remote(steps, step_in[hop].at[relay_d, c], t_send.at[hop, 2, c], t_recv.at[hop, relay_d, c], relay_to, grp),
            ),
        )

    code_sends = {(h, d, c): code_send(h, d, c) for h in range(2) for d in range(2) for c in range(CHUNKS)}

    def send_back(hop, d, c, value):
        codes, step = encode(value)
        code_out[hop][d, c * cut : (c + 1) * cut, :] = codes
        step_out[hop][d, c] = step
        for copy in code_sends[hop, d, c]:
            copy.start()

    def received(hop, d, c):
        code_wait(hop, d, c)
        return decode(code_in[hop][d, c * cut : (c + 1) * cut, :], step_in[hop][d, c])

    middle = near + CHUNKS // 2 * 2 * cut
    for parts, lo, hi in (((0, 1), near, middle), ((2, 3), middle, every)):
        far = term(lo, hi)
        for c in parts:
            for d in range(2):
                at = near + (2 * c + 1 - d) * cut - lo
                send_back(0, d, c, far[at : at + cut, :])
    weigh(0, near)

    across = (((0,), (0,)), ((), ()))
    def query_part(chip):
        lanes = lanes_of(chip)
        value = lax.dot_general(weights[:, lanes], keys[0:every, :], across, preferred_element_type=jnp.float32)
        value = value - lax.dot_general(
            hits_buf[:, lanes], keys[0:rows, :], across, preferred_element_type=jnp.float32
        )
        part[pl.ds(chip * pair, pair)] = value.reshape(pair, rows, width)

    sib_copies = [
        remote(part.at[t], sib_in.at[i], d_send.at[i], d_recv.at[i], blk, sib)
        for i, t in ((0, sib), (1, dia))
    ]
    query_part(1 - chip)
    sib_copies[1].start()
    query_part(chip)
    sib_copies[0].start()
    sib_copies[1].wait_recv()
    x_copies = []
    for i, r in enumerate(query_rows):
        codes, step = encode(part[par, r] + sib_in[1, r])
        codex_out[r, :] = codes
        stepx_out[i] = step
        x_copies.append((
            remote(codex_out.at[r], codex_in.at[r], x_send.at[0, i], x_recv.at[0, i], blk, par),
            remote(stepx_out.at[i], stepx_in.at[i], x_send.at[1, i], x_recv.at[1, i], blk, par),
        ))
    for copy in x_copies[0]:
        copy.start()

    @pl.when(jnp.logical_not(is_relay))
    def _():
        for copy in x_copies[1]:
            copy.start()

    for c in CODE_DETOUR[0]:
        relay(0, c, code_relay)
    home[...] = jnp.dot(weights[0:near, :], every_query, preferred_element_type=jnp.float32)
    home[0:rows, :] -= jnp.dot(hits_buf[...], every_query, preferred_element_type=jnp.float32)
    def pass_home(d, c):
        lo = rows * (2 - d) + c * cut
        send_back(1, d, c, home[lo : lo + cut, :] + received(0, d, c))

    def pass_at_edge(inner):
        for c in range(CHUNKS):
            pass_home(inner, c)
            if c == max(CODE_DETOUR[1]):
                for copy in x_copies[1]:
                    copy.start()
        for c in (2, 3, 0, 1):
            pass_home(1 - inner, c)

    @pl.when(is_last)
    def _():
        pass_at_edge(0)

    @pl.when(is_first)
    def _():
        pass_at_edge(1)

    @pl.when(jnp.logical_not(is_relay))
    def _():
        for c in range(CHUNKS):
            for d in range(2):
                pass_home(d, c)

    for c in CODE_DETOUR[1]:
        relay(1, c, code_relay)
    for c in range(CHUNKS):
        lo = c * cut
        grad_b_out[lo : lo + cut, :] = home[lo : lo + cut, :] + received(1, 0, c) + received(1, 1, c)
        if c == 1:
            sib_copies[0].wait_recv()
            for i, r in enumerate(query_rows):
                for copy in x_copies[i]:
                    copy.wait_recv()
                grad_a_out[r, :] = part[grp, r] + sib_in[0, r] + decode(codex_in[r, :], stepx_in[i])

    for copy in key_sends.values():
        copy.wait_send()
    for pair in code_sends.values():
        for copy in pair:
            copy.wait_send()
    for copy in (*to_par, to_sib, *onward, *pos_copies, *stat_copies, *sib_copies, *x_copies[0], *x_copies[1]):
        copy.wait_send()

    @pl.when(is_relay)
    def _():
        for hop in range(2):
            for c in KEY_DETOUR[hop]:
                for _, leaving in key_relay(hop, c):
                    leaving.wait_send()
            for c in CODE_DETOUR[hop]:
                for _, leaving in code_relay(hop, c):
                    leaving.wait_send()


def body(view_a, view_b, positive):
    rows, width = view_a.shape
    block = rows * GROUPS
    lanes = -(-rows // 128) * 128
    vmem = pl.BlockSpec(memory_space=pltpu.VMEM)
    hbm = pl.BlockSpec(memory_space=pl.ANY)
    dma = pltpu.SemaphoreType.DMA
    f32, bf16, i16 = jnp.float32, jnp.bfloat16, jnp.int16
    codes_out, steps_out = pltpu.VMEM((2, rows, width), i16), pltpu.VMEM((2, CHUNKS, 1, width), f32)
    codes_in, steps_in = pltpu.VMEM((3, rows, width), i16), pltpu.VMEM((3, CHUNKS, 1, width), f32)
    loss, grad_a, grad_b = pl.pallas_call(
        kernel,
        out_shape=(
            pltpu.VMEM((1, rows), f32),
            pltpu.VMEM((rows, width), f32),
            pltpu.VMEM((rows, width), f32),
        ),
        in_specs=[hbm, hbm, vmem],
        out_specs=(vmem, vmem, vmem),
        scratch_shapes=[
            pltpu.VMEM((GROUPS, rows, width), bf16),
            pltpu.VMEM(((WINDOW + 2) * rows, width), bf16),
            pltpu.VMEM((GROUPS, 8, lanes), jnp.int32),
            pltpu.VMEM((GROUPS, 8, block), f32),
            pltpu.VMEM((WINDOW * rows, block), f32),
            pltpu.VMEM((WINDOW * rows, block), bf16),
            pltpu.VMEM((rows, block), bf16),
            pltpu.VMEM(((SPAN + 1) * rows, width), f32),
            codes_out, steps_out, codes_in, steps_in, codes_out, steps_out, codes_in, steps_in,
            pltpu.VMEM((GROUPS, rows, width), f32),
            pltpu.VMEM((2, rows, width), f32),
            pltpu.VMEM((rows, width), i16),
            pltpu.VMEM((2, 1, width), f32),
            pltpu.VMEM((rows, width), i16),
            pltpu.VMEM((2, 1, width), f32),
            dma((2,)),
            dma((2, 3, CHUNKS)), dma((2, 3, CHUNKS)),
            dma((5,)), dma((5,)),
            dma((3,)), dma((3,)),
            dma((3,)), dma((3,)),
            dma((2, 3, CHUNKS)), dma((2, 3, CHUNKS)),
            dma((2, 3, CHUNKS)), dma((2, 3, CHUNKS)),
            dma((2,)), dma((2,)),
            dma((2, 2)), dma((2, 2)),
        ],
        compiler_params=pltpu.CompilerParams(
            collective_id=0, has_side_effects=True, vmem_limit_bytes=53 * 2**20
        ),
        cost_estimate=pl.CostEstimate(
            flops=2 * block * rows * width * 17, bytes_accessed=rows * width * 12,
            transcendentals=2 * WINDOW * rows * block,
        ),
    )(view_a, view_b, positive.reshape(1, rows))
    return loss.reshape(rows), inverse_temp * grad_a, inverse_temp * grad_b


def solution(mesh):
    in_specs = (P(("blk", "grp"), None), P(("blk", "grp"), None), P(("blk", "grp")))
    out_specs = (P(("blk", "grp")), P(("blk", "grp"), None), P(("blk", "grp"), None))
    return jax.shard_map(body, mesh=mesh, in_specs=in_specs, out_specs=out_specs, check_vma=False)
```

```python
import functools

import jax
import jax.numpy as jnp
from jax import lax
from jax.experimental import pallas as pl
from jax.experimental.pallas import tpu as pltpu
from jax.sharding import PartitionSpec as P

SPAN = 2
WINDOW = 2 * SPAN + 1
GROUPS = 4
CHUNKS = 4
KEY_DETOUR = ((0, 1), (0, 1))
CODE_DETOUR = ((0,), (0, 1))
inverse_temp = 20.0
MESH = pl.DeviceIdType.MESH
TOP = 32766.0


def encode(x):
    peak = jnp.max(jnp.abs(x), axis=0, keepdims=True)
    alive = peak > 1e-30
    scale = jnp.where(alive, TOP / jnp.where(alive, peak, 1.0), 0.0)
    codes = jnp.round(x * scale).astype(jnp.int32).astype(jnp.int16)
    return codes, jnp.where(alive, peak * (1.0 / TOP), 0.0)


def decode(codes, step):
    return codes.astype(jnp.int32).astype(jnp.float32) * step


def kernel(
    a_in, b_in, pos_in, loss_out, grad_a_out, grad_b_out,
    queries, keys, pos_buf, stat_buf, scores, weights, hits_buf, home,
    code1_out, step1_out, code1_in, step1_in, code2_out, step2_out, code2_in, step2_in,
    part, sib_in, codex_out, stepx_out, codex_in, stepx_in,
    load_sem, b_send, b_recv, a_send, a_recv, p_send, p_recv, s_send, s_recv,
    c_send, c_recv, t_send, t_recv, d_send, d_recv, x_send, x_recv,
):
    rows, width = a_in.shape
    block = rows * GROUPS
    cut = rows // CHUNKS
    near = (SPAN + 1) * rows
    every = WINDOW * rows
    blk = lax.axis_index("blk")
    grp = lax.axis_index("grp")
    blocks = lax.axis_size("blk")
    right = lax.rem(blk + 1, blocks)
    left = lax.rem(blk + blocks - 1, blocks)
    sib = grp + 1 - 2 * lax.rem(grp, 2)
    par = lax.rem(grp + 2, GROUPS)
    dia = lax.rem(sib + 2, GROUPS)
    peers = (sib, par, dia)

    half = blocks // 2
    spot = lax.rem(blk, half)
    is_last, is_first = spot == half - 1, spot == 0
    is_relay = jnp.logical_or(is_last, is_first)
    detour = (is_last, is_first)
    across_x = lax.rem(blk + half, blocks)
    relay_to = lax.rem(blk + jnp.where(is_last, half + 1, half - 1), blocks)
    relay_d = jnp.where(is_last, 0, 1)

    def route(detours, d, c):
        if c not in detours:
            return False, (right, left)[d]
        return detour[d], jnp.where(detour[d], across_x, (right, left)[d])

    def pick(flag, a, b):
        return b if flag is False else jnp.where(flag, a, b)

    def remote(src, dst, send, recv, to_blk, to_grp):
        return pltpu.make_async_remote_copy(
            src_ref=src, dst_ref=dst, send_sem=send, recv_sem=recv,
            device_id=(to_blk, to_grp), device_id_type=MESH,
        )

    def span(lo, size):
        return pl.ds(pl.multiple_of(lo, 16), size)

    load_b = pltpu.make_async_copy(b_in, keys.at[pl.ds(0, rows)], load_sem.at[0])
    load_a = pltpu.make_async_copy(a_in, queries.at[grp], load_sem.at[1])
    load_b.start()
    load_a.start()

    barrier = pltpu.get_barrier_semaphore()

    def greet(to_blk, to_grp):
        pl.semaphore_signal(barrier, inc=1, device_id=(to_blk, to_grp), device_id_type=MESH)

    greet(right, grp)
    greet(left, grp)
    for peer in peers:
        greet(blk, peer)

    @pl.when(is_relay)
    def _():
        greet(across_x, grp)
        greet(relay_to, grp)

    pos_buf[grp] = jnp.zeros(pos_buf.shape[1:], jnp.int32)
    pos_buf[grp, 0:1, 0:rows] = pos_in[...] - blk * block
    pl.semaphore_wait(barrier, 5 + jnp.where(is_relay, 2, 0))
    load_b.wait()

    def key_place(hop, d, c):
        if hop == 0:
            lands = rows * (1 + d) + c * cut
        else:
            lands = near + (2 * c + d) * cut
        return lands, every + hop * rows + c * cut

    def key_send(hop, d, c):
        src = c * cut if hop == 0 else rows * (1 + d) + c * cut
        direct, held = key_place(hop, d, c)
        by_relay, to_blk = route(KEY_DETOUR[hop], d, c)
        return remote(
            keys.at[pl.ds(src, cut)], keys.at[span(pick(by_relay, held, direct), cut)],
            b_send.at[hop, d, c], b_recv.at[hop, pick(by_relay, 2, d), c], to_blk, grp,
        )

    def key_wait(hop, d, c):
        place = keys.at[pl.ds(key_place(hop, d, c)[0], cut)]
        remote(place, place, b_send.at[hop, d, c], b_recv.at[hop, d, c], right, grp).wait_recv()

    def key_relay(hop, c):
        held = keys.at[pl.ds(key_place(hop, 0, c)[1], cut)]
        lands = jnp.where(is_last, key_place(hop, 0, c)[0], key_place(hop, 1, c)[0])
        return ((
            remote(held, held, b_send.at[hop, 2, c], b_recv.at[hop, 2, c], relay_to, grp),
            remote(held, keys.at[span(lands, cut)], b_send.at[hop, 2, c], b_recv.at[hop, relay_d, c], relay_to, grp),
        ),)

    def relay(hop, c, copies):
        @pl.when(is_relay)
        def _():
            for arriving, _ in copies(hop, c):
                arriving.wait_recv()
            for _, leaving in copies(hop, c):
                leaving.start()

    key_sends = {(h, d, c): key_send(h, d, c) for h in range(2) for d in range(2) for c in range(CHUNKS)}
    middle_row = rows // 2
    query_rows = [pl.ds(i * middle_row, middle_row) for i in range(2)]
    to_par = [
        remote(queries.at[grp, r], queries.at[grp, r], a_send.at[1 + i], a_recv.at[1 + i], blk, par)
        for i, r in enumerate(query_rows)
    ]
    to_sib = remote(queries.at[grp], queries.at[grp], a_send.at[0], a_recv.at[0], blk, sib)
    for c in range(CHUNKS):
        for d in range(2):
            key_sends[0, d, c].start()
    load_a.wait()
    to_sib.start()

    @pl.when(jnp.logical_not(is_relay))
    def _():
        for copy in to_par:
            copy.start()

    pos_copies = [
        remote(pos_buf.at[grp], pos_buf.at[grp], p_send.at[i], p_recv.at[i], blk, peer)
        for i, peer in enumerate(peers)
    ]
    for copy in pos_copies:
        copy.start()

    def take(d, c):
        key_wait(0, d, c)
        key_sends[1, d, c].start()

    def take_at_edge(inner):
        for c in KEY_DETOUR[0]:
            take(inner, c)
            for arriving, leaving in key_relay(0, c):
                arriving.wait_recv()
                leaving.start()
        for copy in to_par:
            copy.start()
        direct = [c for c in range(CHUNKS) if c not in KEY_DETOUR[0]]
        for d, parts in ((inner, direct), (1 - inner, direct), (1 - inner, KEY_DETOUR[0])):
            for c in parts:
                take(d, c)
        for c in KEY_DETOUR[1]:
            for arriving, leaving in key_relay(1, c):
                arriving.wait_recv()
                leaving.start()

    @pl.when(is_last)
    def _():
        take_at_edge(0)

    @pl.when(is_first)
    def _():
        take_at_edge(1)

    @pl.when(jnp.logical_not(is_relay))
    def _():
        for c in range(CHUNKS):
            for d in range(2):
                take(d, c)

    onward = [
        remote(queries.at[par, r], queries.at[par, r], a_send.at[3 + i], a_recv.at[3 + i], blk, sib)
        for i, r in enumerate(query_rows)
    ]
    for copy in pos_copies:
        copy.wait_recv()
    place = jnp.concatenate([pos_buf[t, 0:1, 0:rows] for t in range(GROUPS)], axis=1)
    own_rows = lax.broadcasted_iota(jnp.int32, (rows, block), 0) + grp * rows
    hits = own_rows == place
    hits_buf[...] = jnp.where(hits, 1.0, 0.0).astype(jnp.bfloat16)
    pair = GROUPS // 2
    chip = grp // pair

    def lanes_of(chip):
        return pl.ds(pl.multiple_of(chip * pair * rows, 128), pair * rows)

    def score_near(chip):
        lanes = lanes_of(chip)
        value = inverse_temp * lax.dot_general(
            keys[0:near, :], queries[pl.ds(chip * pair, pair)].reshape(pair * rows, width),
            (((1,), (1,)), ((), ())), preferred_element_type=jnp.float32,
        )
        scores[0:near, lanes] = value
        peak = jnp.max(value, axis=0, keepdims=True)
        stat_buf[grp, 3:4, lanes] = peak
        stat_buf[grp, 4:5, lanes] = jnp.sum(jnp.exp(value - peak), axis=0, keepdims=True)

    to_sib.wait_recv()
    score_near(chip)
    for i in range(2):
        to_par[i].wait_recv()
        onward[i].start()
    for copy in onward:
        copy.wait_recv()
    score_near(1 - chip)

    every_query = queries[...].reshape(block, width)

    def score(lo, hi):
        scores[lo:hi, :] = inverse_temp * lax.dot_general(
            keys[lo:hi, :], every_query, (((1,), (1,)), ((), ())), preferred_element_type=jnp.float32
        )
        peak = jnp.max(scores[lo:hi, :], axis=0, keepdims=True)
        return peak, jnp.sum(jnp.exp(scores[lo:hi, :] - peak), axis=0, keepdims=True)

    def merge(stats):
        peak = functools.reduce(jnp.maximum, [p for p, _ in stats])
        return peak, sum(t * jnp.exp(p - peak) for p, t in stats)

    stats = [(stat_buf[grp, 3:4, :], stat_buf[grp, 4:5, :])]
    matched = jnp.sum(jnp.where(hits, scores[0:rows, :], 0.0), axis=0, keepdims=True)
    last = near + (CHUNKS - 1) * 2 * cut
    for c in range(CHUNKS):
        if c == CHUNKS - 1:
            stats.append(score(near, last))
        for d in range(2):
            key_wait(1, d, c)
    stats.append(score(last, every))
    peak, total = merge(stats)

    stat_buf[grp, 0:1, :] = peak
    stat_buf[grp, 1:2, :] = total
    stat_buf[grp, 2:3, :] = matched
    stat_copies = [
        remote(stat_buf.at[grp], stat_buf.at[grp], s_send.at[i], s_recv.at[i], blk, peer)
        for i, peer in enumerate(peers)
    ]
    for copy in stat_copies:
        copy.start()
    for copy in stat_copies:
        copy.wait_recv()
    peak, total = merge([(stat_buf[t, 0:1, :], stat_buf[t, 1:2, :]) for t in range(GROUPS)])
    lse = peak + jnp.log(total)
    losses = lse - sum(stat_buf[t, 2:3, :] for t in range(GROUPS))
    own_loss = losses[:, 0:rows]
    for t in range(1, GROUPS):
        own_loss = jnp.where(grp == t, losses[:, t * rows : (t + 1) * rows], own_loss)
    loss_out[...] = own_loss

    def weigh(lo, hi):
        weights[lo:hi, :] = jnp.exp(scores[lo:hi, :] - lse).astype(jnp.bfloat16)

    def term(lo, hi):
        weigh(lo, hi)
        return jnp.dot(weights[lo:hi, :], every_query, preferred_element_type=jnp.float32)

    code_out, step_out = (code1_out, code2_out), (step1_out, step2_out)
    code_in, step_in = (code1_in, code2_in), (step1_in, step2_in)

    def code_send(hop, d, c):
        part_rows = pl.ds(c * cut, cut)
        by_relay, to_blk = route(CODE_DETOUR[hop], d, c)
        slot = pick(by_relay, 2, d)
        return (
            remote(
                code_out[hop].at[d, part_rows], code_in[hop].at[slot, part_rows],
                c_send.at[hop, d, c], c_recv.at[hop, slot, c], to_blk, grp,
            ),
            remote(
                step_out[hop].at[d, c], step_in[hop].at[slot, c],
                t_send.at[hop, d, c], t_recv.at[hop, slot, c], to_blk, grp,
            ),
        )

    def code_wait(hop, d, c):
        codes, steps = code_in[hop].at[d, pl.ds(c * cut, cut)], step_in[hop].at[d, c]
        remote(codes, codes, c_send.at[hop, d, c], c_recv.at[hop, d, c], right, grp).wait_recv()
        remote(steps, steps, t_send.at[hop, d, c], t_recv.at[hop, d, c], right, grp).wait_recv()

    def code_relay(hop, c):
        part_rows = pl.ds(c * cut, cut)
        codes, steps = code_in[hop].at[2, part_rows], step_in[hop].at[2, c]
        return (
            (
                remote(codes, codes, c_send.at[hop, 2, c], c_recv.at[hop, 2, c], relay_to, grp),
                remote(codes, code_in[hop].at[relay_d, part_rows], c_send.at[hop, 2, c], c_recv.at[hop, relay_d, c], relay_to, grp),
            ),
            (
                remote(steps, steps, t_send.at[hop, 2, c], t_recv.at[hop, 2, c], relay_to, grp),
                remote(steps, step_in[hop].at[relay_d, c], t_send.at[hop, 2, c], t_recv.at[hop, relay_d, c], relay_to, grp),
            ),
        )

    code_sends = {(h, d, c): code_send(h, d, c) for h in range(2) for d in range(2) for c in range(CHUNKS)}

    def send_back(hop, d, c, value):
        codes, step = encode(value)
        code_out[hop][d, c * cut : (c + 1) * cut, :] = codes
        step_out[hop][d, c] = step
        for copy in code_sends[hop, d, c]:
            copy.start()

    def received(hop, d, c):
        code_wait(hop, d, c)
        return decode(code_in[hop][d, c * cut : (c + 1) * cut, :], step_in[hop][d, c])

    middle = near + CHUNKS // 2 * 2 * cut
    for parts, lo, hi in (((0, 1), near, middle), ((2, 3), middle, every)):
        far = term(lo, hi)
        for c in parts:
            for d in range(2):
                at = near + (2 * c + 1 - d) * cut - lo
                send_back(0, d, c, far[at : at + cut, :])
    weigh(0, near)

    across = (((0,), (0,)), ((), ()))
    def query_part(chip):
        lanes = lanes_of(chip)
        value = lax.dot_general(weights[:, lanes], keys[0:every, :], across, preferred_element_type=jnp.float32)
        value = value - lax.dot_general(
            hits_buf[:, lanes], keys[0:rows, :], across, preferred_element_type=jnp.float32
        )
        part[pl.ds(chip * pair, pair)] = value.reshape(pair, rows, width)

    sib_copies = [
        remote(part.at[t], sib_in.at[i], d_send.at[i], d_recv.at[i], blk, sib)
        for i, t in ((0, sib), (1, dia))
    ]
    query_part(1 - chip)
    sib_copies[1].start()
    query_part(chip)
    sib_copies[0].start()
    sib_copies[1].wait_recv()
    x_copies = []
    for i, r in enumerate(query_rows):
        codes, step = encode(part[par, r] + sib_in[1, r])
        codex_out[r, :] = codes
        stepx_out[i] = step
        x_copies.append((
            remote(codex_out.at[r], codex_in.at[r], x_send.at[0, i], x_recv.at[0, i], blk, par),
            remote(stepx_out.at[i], stepx_in.at[i], x_send.at[1, i], x_recv.at[1, i], blk, par),
        ))
    for copy in x_copies[0]:
        copy.start()

    @pl.when(jnp.logical_not(is_relay))
    def _():
        for copy in x_copies[1]:
            copy.start()

    for c in CODE_DETOUR[0]:
        relay(0, c, code_relay)
    home[...] = jnp.dot(weights[0:near, :], every_query, preferred_element_type=jnp.float32)
    home[0:rows, :] -= jnp.dot(hits_buf[...], every_query, preferred_element_type=jnp.float32)
    def pass_home(d, c):
        lo = rows * (2 - d) + c * cut
        send_back(1, d, c, home[lo : lo + cut, :] + received(0, d, c))

    def pass_at_edge(inner):
        for c in range(CHUNKS):
            pass_home(inner, c)
            if c == max(CODE_DETOUR[1]):
                for copy in x_copies[1]:
                    copy.start()
        for c in (2, 3, 0, 1):
            pass_home(1 - inner, c)

    @pl.when(is_last)
    def _():
        pass_at_edge(0)

    @pl.when(is_first)
    def _():
        pass_at_edge(1)

    @pl.when(jnp.logical_not(is_relay))
    def _():
        for c in range(CHUNKS):
            for d in range(2):
                pass_home(d, c)

    for c in CODE_DETOUR[1]:
        relay(1, c, code_relay)
    for c in range(CHUNKS):
        lo = c * cut
        grad_b_out[lo : lo + cut, :] = home[lo : lo + cut, :] + received(1, 0, c) + received(1, 1, c)
        if c == 1:
            sib_copies[0].wait_recv()
            for i, r in enumerate(query_rows):
                for copy in x_copies[i]:
                    copy.wait_recv()
                grad_a_out[r, :] = part[grp, r] + sib_in[0, r] + decode(codex_in[r, :], stepx_in[i])

    for copy in key_sends.values():
        copy.wait_send()
    for pair in code_sends.values():
        for copy in pair:
            copy.wait_send()
    for copy in (*to_par, to_sib, *onward, *pos_copies, *stat_copies, *sib_copies, *x_copies[0], *x_copies[1]):
        copy.wait_send()

    @pl.when(is_relay)
    def _():
        for hop in range(2):
            for c in KEY_DETOUR[hop]:
                for _, leaving in key_relay(hop, c):
                    leaving.wait_send()
            for c in CODE_DETOUR[hop]:
                for _, leaving in code_relay(hop, c):
                    leaving.wait_send()


def body(view_a, view_b, positive):
    rows, width = view_a.shape
    block = rows * GROUPS
    lanes = -(-rows // 128) * 128
    vmem = pl.BlockSpec(memory_space=pltpu.VMEM)
    hbm = pl.BlockSpec(memory_space=pl.ANY)
    dma = pltpu.SemaphoreType.DMA
    f32, bf16, i16 = jnp.float32, jnp.bfloat16, jnp.int16
    codes_out, steps_out = pltpu.VMEM((2, rows, width), i16), pltpu.VMEM((2, CHUNKS, 1, width), f32)
    codes_in, steps_in = pltpu.VMEM((3, rows, width), i16), pltpu.VMEM((3, CHUNKS, 1, width), f32)
    loss, grad_a, grad_b = pl.pallas_call(
        kernel,
        out_shape=(
            pltpu.VMEM((1, rows), f32),
            pltpu.VMEM((rows, width), f32),
            pltpu.VMEM((rows, width), f32),
        ),
        in_specs=[hbm, hbm, vmem],
        out_specs=(vmem, vmem, vmem),
        scratch_shapes=[
            pltpu.VMEM((GROUPS, rows, width), bf16),
            pltpu.VMEM(((WINDOW + 2) * rows, width), bf16),
            pltpu.VMEM((GROUPS, 8, lanes), jnp.int32),
            pltpu.VMEM((GROUPS, 8, block), f32),
            pltpu.VMEM((WINDOW * rows, block), f32),
            pltpu.VMEM((WINDOW * rows, block), bf16),
            pltpu.VMEM((rows, block), bf16),
            pltpu.VMEM(((SPAN + 1) * rows, width), f32),
            codes_out, steps_out, codes_in, steps_in, codes_out, steps_out, codes_in, steps_in,
            pltpu.VMEM((GROUPS, rows, width), f32),
            pltpu.VMEM((2, rows, width), f32),
            pltpu.VMEM((rows, width), i16),
            pltpu.VMEM((2, 1, width), f32),
            pltpu.VMEM((rows, width), i16),
            pltpu.VMEM((2, 1, width), f32),
            dma((2,)),
            dma((2, 3, CHUNKS)), dma((2, 3, CHUNKS)),
            dma((5,)), dma((5,)),
            dma((3,)), dma((3,)),
            dma((3,)), dma((3,)),
            dma((2, 3, CHUNKS)), dma((2, 3, CHUNKS)),
            dma((2, 3, CHUNKS)), dma((2, 3, CHUNKS)),
            dma((2,)), dma((2,)),
            dma((2, 2)), dma((2, 2)),
        ],
        compiler_params=pltpu.CompilerParams(
            collective_id=0, has_side_effects=True, vmem_limit_bytes=53 * 2**20
        ),
        cost_estimate=pl.CostEstimate(
            flops=2 * block * rows * width * 17, bytes_accessed=rows * width * 12,
            transcendentals=2 * WINDOW * rows * block,
        ),
    )(view_a, view_b, positive.reshape(1, rows))
    return loss.reshape(rows), inverse_temp * grad_a, inverse_temp * grad_b


def solution(mesh):
    in_specs = (P(("blk", "grp"), None), P(("blk", "grp"), None), P(("blk", "grp")))
    out_specs = (P(("blk", "grp")), P(("blk", "grp"), None), P(("blk", "grp"), None))
    return jax.shard_map(body, mesh=mesh, in_specs=in_specs, out_specs=out_specs, check_vma=False)
```
